32 devices in a mesh: gx: 4 (over z), gy: 8 (over y, x, core).
Axes of the slice: x: 2, y: 2, z: 4, core: 2. Of those that a mesh axis runs over, the one named last changes fastest.
Arguments:
- wavefield: float32 [9, 56, 4096], P(None, None, ('gx', 'gy')), may hold values from -6 to 6
- star_mats: float32 [3, 9, 9, 4096], P(None, None, None, ('gx', 'gy')), may hold values from -1 to 1
- flux_own: float32 [4, 9, 9, 4096], P(None, None, None, ('gx', 'gy')), may hold values from -0.8 to 0.8
- flux_nbr: float32 [4, 9, 9, 4096], P(None, None, None, ('gx', 'gy')), may hold values from -0.8 to 0.8
- stiffness: float32 [3, 56, 56], replicated, may hold values from -0.75 to 0.75
- face_proj: float32 [4, 21, 56], replicated, may hold values from -0.75 to 0.75
- lift_mats: float32 [4, 56, 21], replicated, may hold values from -1.25 to 1.25
- cluster: int32 [4096], P(('gx', 'gy')), may hold values from 0 to 1
- yield_stress: float32 [4096], P(('gx', 'gy')), may hold values from 0.5 to 5
- plastic_mask: int32 [4096], P(('gx', 'gy')), may hold values from 0 to 1
- face_source: int32 [4, 4096], P(None, ('gx', 'gy')), may hold values from 0 to 639, as said below
- send_faces: int32 [128, 32], P(('gx', 'gy')), may hold values from 0 to 511, as said below
- fault_faces: int32 [32, 64], P(('gx', 'gy')), may hold values from 0 to 511, as said below
- fault_owner: int32 [2048, 1], P(('gx', 'gy')), may hold values from 0 to 7; in each aligned block of 64 rows (0 to 63, 64 to 127, ...) at most 16 rows name the same one
- fault_slip: float32 [4096], P(('gx', 'gy')), may hold values from 0 to 1
- cohesion: float32 [4096], P(('gx', 'gy')), may hold values from 0.1 to 1
- slip_flag: int32 [4096], P(('gx', 'gy')), may hold values from 0 to 1
Outputs:
- wavefield_out: float32 [9, 56, 4096], P(None, None, ('gx', 'gy'))
- slip_out: float32 [4096], P(('gx', 'gy'))
The draws below stay inside these ranges and needn't reach their ends.
Inputs may be any that keep to these rules, and one draw needn't show every extreme that they name: `face_source`: entries below 512 name the partition's own faces; every received slot is named by exactly one face of its partition. `send_faces`: entries of one row are distinct. `fault_faces`: entries of one partition are distinct. `fault_owner`: among the fault faces of one partition at most 16 name the same owner.
All inputs are finite; a program needn't handle non-finite values.
Results may differ from the reference program's by a relative error of at most 0.0001.
Values sent between devices are 32-bit elements; how exact they have to be, the bound alone decides.
A program may use at most 64 MiB of HBM per device.

```python
import math
import jax
import jax.numpy as jnp
import numpy as np
from jax import lax

VARS = 9
MODES = 56
FACE_PTS = 21
ORDER = 6
CYCLES = 1
E_DEV = 128
SLOTS = 32
FAULT_DEV = 64
PARTITIONS = 32
ELEMS = 4096
CAP = 16
OWNER_SLOTS = 4096
N_GX = 4
N_GY = 8


def face_rows(key):
    keys = jax.random.split(key, 2)
    shuffled = jax.random.permutation(keys[0], 4 * E_DEV).astype(jnp.int32)
    local_rows = jax.random.randint(keys[1], (4 * E_DEV,), 0, 4 * E_DEV).astype(jnp.int32)
    slot_rows = 4 * E_DEV + jnp.arange(4 * SLOTS, dtype=jnp.int32)
    return local_rows.at[shuffled[:4 * SLOTS]].set(slot_rows)


def topped_choice(key, amount):
    shuffled = jax.random.permutation(key, 4 * E_DEV).astype(jnp.int32)
    where_top = jnp.argmax(shuffled)
    leading = shuffled[0]
    shuffled = shuffled.at[where_top].set(leading).at[0].set(4 * E_DEV - 1)
    return shuffled[:amount]


def draw_face_source(key, part):
    keys = jax.random.split(jax.random.fold_in(key, 11), PARTITIONS)
    stacked = jax.vmap(face_rows)(keys)
    return jnp.transpose(stacked.reshape(PARTITIONS, 4, E_DEV), (1, 0, 2)).reshape(4, PARTITIONS * E_DEV).astype(jnp.int32)


def draw_send_faces(key, part):
    keys = jax.random.split(jax.random.fold_in(key, 23), PARTITIONS)
    stacked = jax.vmap(lambda single: topped_choice(single, 4 * SLOTS))(keys)
    return stacked.reshape(PARTITIONS * 4, SLOTS).astype(jnp.int32)


def draw_fault_faces(key, part):
    keys = jax.random.split(jax.random.fold_in(key, 37), PARTITIONS)
    stacked = jax.vmap(lambda single: topped_choice(single, FAULT_DEV))(keys)
    return stacked.reshape(PARTITIONS, FAULT_DEV).astype(jnp.int32)


def set_ends(entries, key, least, largest):
    longest = entries.shape.index(max(entries.shape))
    spots = []
    for shift in (0, 1):
        where = [jax.random.randint(jax.random.fold_in(key, axis), (), 0, length) for axis, length in enumerate(entries.shape)]
        where[longest] = (where[longest] + shift) % entries.shape[longest]
        spots.append(tuple(where))
    return entries.at[spots[0]].set(least).at[spots[1]].set(largest)


def level_of(rng, dims, shards, smallest, top_value):
    factor_of = 1.0
    for axis_at, blocks in shards:
        draws = jax.random.uniform(jax.random.fold_in(jax.random.fold_in(rng, 6), axis_at), (blocks,), jnp.float32, smallest / len(shards), top_value / len(shards))
        factor_of = factor_of * jnp.repeat(jnp.exp(draws), dims[axis_at] // blocks).reshape((-1,) + (1,) * (len(dims) - 1 - axis_at))
    return factor_of


def shared_out(own_key, own, number, rows, count, top, limit, slope):
    order = jax.random.permutation(own_key, count)
    crowded, usual = shares(count, rows * top, limit, slope, True), shares(count, rows * top, limit, slope, False)
    places = jnp.arange(count)

    def named(sizes, rotation):
        used = int((sizes > 0).sum())
        fixed = max(1, used // 4)
        moved = fixed + (places - fixed + rotation * (used - fixed)) % max(1, count - fixed)
        return jnp.zeros((count,), jnp.int32).at[order[jnp.where(places < fixed, places, moved)]].set(jnp.asarray(sizes, jnp.int32))

    sizes = jnp.where(number % 4 == 0, named(crowded, number // 4), named(usual, number - number // 4 - 1))
    mixed = jax.random.permutation(jax.random.fold_in(own, 3), count)
    donor, sink = mixed[0:count // 2 * 2:2], mixed[1:count // 2 * 2:2]
    room = jnp.minimum(sizes[donor] - 1, limit - sizes[sink]) // 2
    room = jnp.where((donor == order[0]) | (sink == order[0]) | (sizes[sink] == 0), 0, jnp.maximum(room, 0))
    moved = jax.random.randint(jax.random.fold_in(own, 4), (count // 2,), 0, 1 << 20) % (room + 1)
    sizes = sizes.at[donor].add(-moved).at[sink].add(moved)
    items = jnp.searchsorted(jnp.cumsum(sizes), jnp.arange(rows * top), side="right").astype(jnp.int32)
    grid = items.reshape(top, rows).T
    grid = grid[jax.random.permutation(jax.random.fold_in(own, 1), rows)]
    rotation = jax.random.randint(jax.random.fold_in(own, 2), (rows, 1), 0, top)
    return jnp.take_along_axis(grid, (jnp.arange(top)[None, :] + rotation) % top, axis=1)


def shares(number_of, total, most, lean, full):
    loads = [(1 << 20) // math.isqrt(grade ** lean) + 1 for grade in range(1, number_of + 1)]
    largest = most if full else min(most, max(-(-total // number_of), total * loads[0] // sum(loads)))
    least = 1 if total - largest >= number_of - 1 else 0
    given, surplus = [largest] + [least] * (number_of - 1), total - largest - least * (number_of - 1)
    while surplus > 0:
        free = [i for i in range(1, number_of) if given[i] < largest] or [i for i in range(1, number_of) if given[i] < most]
        mass, budget = sum([loads[i] for i in free]), surplus
        for i in free:
            extra = min(most - given[i], max(1, budget * loads[i] // mass), surplus)
            given[i] = given[i] + extra
            surplus = surplus - extra
    return np.array(given)


def centred(stream_key, dims, scale, most, cuts=(), held_as=jnp.bfloat16):
    values = jax.random.normal(stream_key, dims, jnp.float32) * scale
    if len(cuts) > 0:
        values = level_of(stream_key, dims, cuts, -0.22, 0.18) * values
    return jnp.clip(values, min=-most, max=most).astype(held_as)


def setup_inputs(seed: int = 0) -> dict:
    arg_keys = jax.random.split(jax.random.key(seed), 18)
    wavefield = centred(arg_keys[0], (VARS, MODES, ELEMS), 1.0, 6.0, ((2, 32),), jnp.float32)
    star_mats = centred(arg_keys[1], (3, VARS, VARS, ELEMS), 0.15, 1.0, ((3, 32),), jnp.float32)
    flux_own = centred(arg_keys[2], (4, VARS, VARS, ELEMS), 0.1, 0.8, ((3, 32),), jnp.float32)
    flux_nbr = centred(arg_keys[3], (4, VARS, VARS, ELEMS), 0.1, 0.8, ((3, 32),), jnp.float32)
    stiffness = centred(arg_keys[4], (3, MODES, MODES), MODES ** -0.5, 0.75, (), jnp.float32)
    face_proj = centred(arg_keys[5], (4, FACE_PTS, MODES), MODES ** -0.5, 0.75, (), jnp.float32)
    lift_mats = centred(arg_keys[6], (4, MODES, FACE_PTS), FACE_PTS ** -0.5, 1.25, (), jnp.float32)
    cluster = set_ends(jax.random.randint(arg_keys[7], (ELEMS,), 0, 2), jax.random.fold_in(arg_keys[7], 1), 0, 1).astype(jnp.int32)
    yield_stress = jnp.clip(jnp.exp(math.log(5.0) - 2.3025851 * jax.random.uniform(arg_keys[8], (ELEMS,), jnp.float32) ** level_of(arg_keys[8], (ELEMS,), ((0, 32),), -0.2, 0.2)), 0.5, 5.0)
    plastic_mask = set_ends(jax.random.randint(arg_keys[9], (ELEMS,), 0, 2), jax.random.fold_in(arg_keys[9], 1), 0, 1).astype(jnp.int32)
    face_source = draw_face_source(jax.random.fold_in(arg_keys[17], 71), 0)
    send_faces = draw_send_faces(jax.random.fold_in(arg_keys[17], 71), 0)
    fault_faces = draw_fault_faces(jax.random.fold_in(arg_keys[17], 71), 0)
    fault_owner_keys = jax.random.split(jax.random.fold_in(arg_keys[13], 1), (PARTITIONS * FAULT_DEV) // FAULT_DEV)
    fault_owner_turns = jax.random.permutation(jax.random.fold_in(arg_keys[13], 3), (PARTITIONS * FAULT_DEV) // FAULT_DEV)
    fault_owner = jax.vmap(lambda own, number: shared_out(jax.random.fold_in(arg_keys[13], 2), own, number, FAULT_DEV, N_GY, 1, CAP, 2))(fault_owner_keys, fault_owner_turns).reshape((PARTITIONS * FAULT_DEV, 1))
    fault_slip = jnp.clip(1.0 * jax.random.uniform(arg_keys[14], (OWNER_SLOTS,), jnp.float32) ** level_of(arg_keys[14], (OWNER_SLOTS,), ((0, 32),), -0.2, 0.2), 0.0, 1.0)
    cohesion = jnp.clip(jnp.exp(math.log(1.0) - 2.3025851 * jax.random.uniform(arg_keys[15], (OWNER_SLOTS,), jnp.float32) ** level_of(arg_keys[15], (OWNER_SLOTS,), ((0, 32),), -0.2, 0.2)), 0.1, 1.0)
    slip_flag = set_ends(jax.random.randint(arg_keys[16], (OWNER_SLOTS,), 0, 2), jax.random.fold_in(arg_keys[16], 1), 0, 1).astype(jnp.int32)
    return dict(wavefield=wavefield, star_mats=star_mats, flux_own=flux_own, flux_nbr=flux_nbr, stiffness=stiffness, face_proj=face_proj, lift_mats=lift_mats, cluster=cluster, yield_stress=yield_stress, plastic_mask=plastic_mask, face_source=face_source, send_faces=send_faces, fault_faces=fault_faces, fault_owner=fault_owner, fault_slip=fault_slip, cohesion=cohesion, slip_flag=slip_flag)


highest = lax.Precision.HIGHEST
picked_vars = (0, 3, 5, 6, 7, 8)

def vars_mix(mats, field):
    total = mats[:, 0][:, None] * field[0][None]
    for source in range(1, field.shape[0]):
        total = total + mats[:, source][:, None] * field[source][None]
    return total

def face_mix(mats_one, trace_one, mats_two, trace_two):
    total = 0.0
    for source in range(trace_one.shape[0]):
        left = jnp.transpose(mats_one[:, :, source], (1, 0, 2))[:, None]
        right = jnp.transpose(mats_two[:, :, source], (1, 0, 2))[:, None]
        total = total + left * trace_one[source][None] + right * trace_two[source][None]
    return total

def predict(wavefield, star_mats, stiffness):
    deriv = wavefield
    early = wavefield
    late = wavefield
    factor = 1.0
    for power in range(2, ORDER + 1):
        factor = factor * power
        change = 0.0
        for axis_dir in range(3):
            mixed = vars_mix(star_mats[axis_dir], deriv)
            change = change + jnp.einsum('nm,vmx->vnx', stiffness[axis_dir], mixed, precision=highest)
        deriv = -change
        early = early + deriv / factor
        late = late + deriv * ((2.0 ** power - 1.0) / factor)
    return (early, late)

def volume(integral, star_mats, stiffness):
    total = 0.0
    for axis_dir in range(3):
        mixed = vars_mix(star_mats[axis_dir], integral)
        total = total + jnp.einsum('mn,vmx->vnx', stiffness[axis_dir], mixed, precision=highest)
    return total

def godunov(picked):
    stacked = []
    for component in range(3):
        stacked.append(0.5 * (picked[component] + picked[6 + component]) + 0.5 * (picked[9 + component] - picked[3 + component]))
    return jnp.stack(stacked)

def friction(state, slip_state, cohesion, slip_flag):
    weaken = jnp.minimum(slip_state / 0.5, 1.0)
    coeff = 0.6 - 0.3 * weaken
    strength = cohesion + coeff * jnp.maximum(-state[0], 0.0)
    magnitude = jnp.sqrt(state[1] * state[1] + state[2] * state[2])
    ratio = jnp.where(slip_flag == 1, strength / jnp.maximum(magnitude, strength), 1.0)
    change = jnp.stack([state[1] * (ratio - 1.0), state[2] * (ratio - 1.0)])
    slip_new = slip_state + lax.optimization_barrier(jnp.mean(magnitude * (1.0 - ratio), axis=0))
    return (change, slip_new)

def plastic(wavefield, plastic_mask, yield_stress):
    mean_stress = (wavefield[0] + wavefield[1] + wavefield[2]) / 3.0
    deviator = wavefield[0:3] - mean_stress
    shear = wavefield[3:6]
    second = (lax.optimization_barrier(jnp.sum(deviator * deviator, axis=(0, 1))) + 2.0 * lax.optimization_barrier(jnp.sum(shear * shear, axis=(0, 1)))) / (2.0 * wavefield.shape[1])
    equiv = jnp.sqrt(second + 1e-06)
    factor = 1.0 - plastic_mask.astype(jnp.float32) * 0.5 * jnp.maximum(1.0 - yield_stress / equiv, 0.0)
    return jnp.concatenate([mean_stress + factor * deviator, factor * shear, wavefield[6:]], axis=0)

def reference(wavefield, star_mats, flux_own, flux_nbr, stiffness, face_proj, lift_mats, cluster, yield_stress, plastic_mask, face_source, send_faces, fault_faces, fault_owner, fault_slip, cohesion, slip_flag):
    parts = N_GX * N_GY
    elems = E_DEV
    width = VARS * FACE_PTS
    is_fine = (cluster == 0)[None, None, :]
    is_coarse = (cluster == 1)[None, None, :]
    owners = fault_owner[:, 0].reshape(parts, FAULT_DEV)
    onehot = (owners[:, :, None] == jnp.arange(N_GY, dtype=jnp.int32)[None, None, :]).astype(jnp.int32)
    before = jnp.cumsum(onehot, axis=1) - onehot
    order_rank = lax.optimization_barrier(jnp.sum(before * onehot, axis=2))
    row_x = (jnp.arange(parts, dtype=jnp.int32) // N_GY)[:, None]
    row_y = (jnp.arange(parts, dtype=jnp.int32) % N_GY)[:, None]
    slot_ids = ((row_x * N_GY + owners) * (N_GY * CAP) + row_y * CAP + order_rank).reshape(-1)
    face_index = fault_faces // elems
    elem_index = jnp.arange(parts, dtype=jnp.int32)[:, None] * elems + fault_faces % elems
    sources = face_source.reshape(4, parts, elems).transpose(1, 0, 2).reshape(parts, 4 * elems)
    sends = send_faces.reshape(parts, 4 * SLOTS)
    chosen = jnp.array(picked_vars, dtype=jnp.int32)

    def advance(integral, slip_state):
        own_traces = jnp.einsum('fjm,vmx->vjfx', face_proj, integral, precision=highest)
        own_table = own_traces.reshape(width, 4, parts, elems).transpose(0, 2, 1, 3).reshape(width, parts, 4 * elems)
        outgoing = jnp.take_along_axis(own_table, sends[None], axis=2).reshape(width, N_GX, N_GY, 4, SLOTS)
        received = jnp.stack([jnp.roll(outgoing[..., 1, :], 1, axis=1), jnp.roll(outgoing[..., 0, :], -1, axis=1), jnp.roll(outgoing[..., 3, :], 1, axis=2), jnp.roll(outgoing[..., 2, :], -1, axis=2)], axis=3)
        table = jnp.concatenate([own_table, received.reshape(width, parts, 4 * SLOTS)], axis=2)
        nbr_table = jnp.take_along_axis(table, sources[None], axis=2)
        nbr_traces = nbr_table.reshape(VARS, FACE_PTS, parts, 4, elems).transpose(0, 1, 3, 2, 4).reshape(VARS, FACE_PTS, 4, parts * elems)
        flux = face_mix(flux_own, own_traces, flux_nbr, nbr_traces)
        minus_side = jnp.take_along_axis(own_table, fault_faces[None], axis=2).reshape(VARS, FACE_PTS, parts * FAULT_DEV)
        plus_side = jnp.take_along_axis(nbr_table, fault_faces[None], axis=2).reshape(VARS, FACE_PTS, parts * FAULT_DEV)
        picked = jnp.concatenate([minus_side[chosen], plus_side[chosen]], axis=0)
        state = godunov(picked)
        slot_state = jnp.zeros((3, FACE_PTS, OWNER_SLOTS), jnp.float32).at[:, :, slot_ids].set(state)
        change, slip_new = friction(slot_state, slip_state, cohesion, slip_flag)
        back = change[:, :, slot_ids].reshape(2, FACE_PTS, parts, FAULT_DEV)
        flux = flux.at[3, :, face_index, elem_index].add(jnp.transpose(back[0], (1, 2, 0)))
        flux = flux.at[5, :, face_index, elem_index].add(jnp.transpose(back[1], (1, 2, 0)))
        increment = volume(integral, star_mats, stiffness) - jnp.einsum('fmj,vjfx->vmx', lift_mats, flux, precision=highest)
        return (increment, slip_new)
    slip_state = fault_slip
    for cycle_index in range(CYCLES):
        early, late = predict(wavefield, star_mats, stiffness)
        first_step, slip_state = advance(early, slip_state)
        carried = jnp.where(is_coarse, first_step, 0.0)
        midway = jnp.where(is_fine, plastic(wavefield + first_step, plastic_mask, yield_stress), wavefield)
        renewed, unused = predict(midway, star_mats, stiffness)
        second_step, slip_state = advance(jnp.where(is_coarse, late, renewed), slip_state)
        wavefield = plastic(midway + second_step + carried, plastic_mask, yield_stress)
    return (wavefield, slip_state)
```

```python
import functools
import math

import jax
import jax.numpy as jnp
from jax import lax
from jax.experimental import pallas as pl
from jax.experimental.pallas import tpu as pltpu
from jax.sharding import PartitionSpec as P

VARS = 9
ORDER = 6
HIGHEST = lax.Precision.HIGHEST
F32 = jnp.float32
BF16 = jnp.bfloat16


def up8(n):
    return -(-n // 8) * 8


def iota_f(shape, axis):
    return lax.broadcasted_iota(jnp.int32, shape, axis).astype(F32)


def dot(a, b):
    return jnp.dot(a, b, preferred_element_type=F32)


def low_part(x):
    return x - x.astype(BF16).astype(F32)


def two_parts(x):
    return jnp.concatenate([x, low_part(x)], axis=0).astype(BF16)


def dot_split(mat, data):
    rows = mat.shape[0]
    top = dot(two_parts(mat), data.astype(BF16))
    return top[:rows] + (top[rows:] + dot(mat.astype(BF16), low_part(data).astype(BF16)))


def pick(parts, select):
    rows = parts.shape[0] // 2
    both = dot(parts, select)
    return both[:rows] + both[rows:]


def kernel(
    cfg,
    wave,
    star,
    own_mats,
    nbr_mats,
    stiff,
    stiff_t,
    proj,
    lift,
    cluster,
    yield_stress,
    mask,
    source,
    sends,
    faults,
    owners,
    slip0,
    cohesion,
    flag,
    out,
    slip_out,
    deriv,
    early,
    late,
    mid,
    inc,
    carried,
    mix,
    own_tab,
    nbr_tab,
    flux,
    select,
    send_select,
    fault_select,
    slots,
    par,
    face_par,
    moved,
    ret,
    got,
    packs,
    recs,
    table_in,
    par_send,
    par_recv,
    ret_send,
    ret_recv,
    tr_send,
    tr_recv,
):
    nx, ny, points = cfg
    modes, elems = wave.shape[1:]
    rows = up8(points)
    faces = 4 * elems
    slot_count = sends.shape[1] // 4
    group = packs.shape[2]
    table_rows = VARS * rows
    cap = slip0.shape[1] // ny
    ix, iy = lax.axis_index("gx"), lax.axis_index("gy")
    x_up = (lax.rem(ix + 1, nx), iy)
    x_down = (lax.rem(ix + nx - 1, nx), iy)
    y_up = (ix, lax.rem(iy + 1, ny))
    y_down = (ix, lax.rem(iy + ny - 1, ny))
    MESH = pl.DeviceIdType.MESH

    def peer(step):
        return (ix, lax.rem(iy + step, ny))

    barrier = pltpu.get_barrier_semaphore()
    for target in [x_up, x_down] + [peer(t) for t in range(1, ny)]:
        pl.semaphore_signal(barrier, inc=1, device_id=target, device_id_type=MESH)

    me = iy.astype(F32)
    table_size = select.shape[0]
    for f in range(4):
        want = source[f : f + 1, :].astype(F32)
        hit = iota_f((table_size, elems), 0) == want
        select[:, f * elems : (f + 1) * elems] = jnp.where(hit, 1.0, 0.0).astype(BF16)
    hit = iota_f((faces, 4 * slot_count), 0) == sends[...].astype(F32)
    send_select[...] = jnp.where(hit, 1.0, 0.0).astype(BF16)
    count = faults.shape[1]
    hit = iota_f((faces, count), 0) == faults[...].astype(F32)
    fault_select[...] = jnp.where(hit, 1.0, 0.0)
    owner_col = owners[...].astype(F32)
    r, c = iota_f((count, count), 0), iota_f((count, count), 1)
    owner_row = jnp.sum(jnp.where(r == c, owner_col, 0.0), axis=0, keepdims=True)
    same = jnp.where((owner_col == owner_row) & (r < c), 1.0, 0.0)
    rank = jnp.sum(same, axis=0, keepdims=True)
    slot_row = me * cap + rank
    slots[...] = jnp.where(iota_f((slip0.shape[1], count), 0) == slot_row, 1.0, 0.0)
    away = owner_row - me
    ahead = jnp.where(away < 0, away + ny, away)
    behind = jnp.where(away > 0, ny - away, -away)

    def mix_all(src, field):
        def one_dir(d, carry):
            at = pl.ds(pl.multiple_of(d * modes, 8), modes)
            for first in range(0, VARS, 3):
                accs = [None] * 3
                for s in range(VARS):
                    value = field[s]
                    for k in range(3):
                        term = star[d, first + k, s : s + 1, :] * value
                        accs[k] = term if s == 0 else accs[k] + term
                for k in range(3):
                    mix[at, (first + k) * elems : (first + k + 1) * elems] = accs[k]
            return carry

        lax.fori_loop(0, 3, one_dir, 0)

    def predict(src, with_late):
        for v in range(VARS):
            deriv[v] = src[v]
            early[v] = src[v]
            if with_late:
                late[v] = src[v]

        def one_power(power, carry):
            scale_early = jnp.float32(0.0)
            scale_late = jnp.float32(0.0)
            for p in range(2, ORDER + 1):
                scale_early = jnp.where(power == p, 1.0 / math.factorial(p), scale_early)
                scale_late = jnp.where(
                    power == p, (2.0**p - 1.0) / math.factorial(p), scale_late
                )
            mix_all(None, deriv)
            change = dot_split(stiff[...], mix[...])
            for v in range(VARS):
                step = -change[:, v * elems : (v + 1) * elems]
                deriv[v] = step
                early[v] += step * scale_early
                if with_late:
                    late[v] += step * scale_late
            return carry

        lax.fori_loop(2, ORDER + 1, one_power, 0)

    def advance(field, turn):
        flat = jnp.concatenate([field[v] for v in range(VARS)], axis=1)
        traces = dot_split(proj[...], flat)
        for v in range(VARS):
            for f in range(4):
                own_tab[v * rows : (v + 1) * rows, f * elems : (f + 1) * elems] = traces[
                    f * rows : (f + 1) * rows, v * elems : (v + 1) * elems
                ]
        own_parts = two_parts(own_tab[...])
        table_in[table_rows:, :] = jnp.zeros((4 * group - table_rows, 4 * slot_count), F32)
        table_in[0:table_rows, :] = pick(own_parts, send_select[...])
        lane_group = lax.broadcasted_iota(jnp.int32, (group, 4 * slot_count), 1) // slot_count
        copies = []
        for q, target in enumerate([x_up, x_down, y_up, y_down]):
            packed = jnp.zeros((group, 4 * slot_count), F32)
            for g in range(4):
                piece = table_in[g * group : (g + 1) * group, :]
                shift = ((g - q) % 4) * slot_count
                if shift:
                    piece = pltpu.roll(piece, shift, 1)
                packed = jnp.where(lane_group == g, piece, packed)
            packs[turn, q] = packed
            copy = pltpu.make_async_remote_copy(
                src_ref=packs.at[turn, q],
                dst_ref=recs.at[turn, q],
                send_sem=tr_send.at[turn, q],
                recv_sem=tr_recv.at[turn, q],
                device_id=target,
                device_id_type=MESH,
            )
            copy.start()
            copies.append(copy)

        mix_all(None, field)
        volume = dot_split(stiff_t[...], mix[...])
        for v in range(VARS):
            inc[v] = volume[:, v * elems : (v + 1) * elems]
        nbr_tab[...] = pick(own_parts, select[0:faces, :])

        def own_flux(f, carry):
            lanes = pl.ds(pl.multiple_of(f * elems, elems), elems)
            at = pl.ds(pl.multiple_of(f * rows, 8), rows)
            accs = [None] * VARS
            for s in range(VARS):
                value = own_tab[s * rows : (s + 1) * rows, lanes]
                for i in range(VARS):
                    term = own_mats[f, i, s : s + 1, :] * value
                    accs[i] = term if s == 0 else accs[i] + term
            for i in range(VARS):
                flux[at, i * elems : (i + 1) * elems] = accs[i]
            return carry

        lax.fori_loop(0, 4, own_flux, 0)
        if turn == 0:
            for copy in par_copies:
                copy.wait_recv()
            chosen = jnp.dot(
                par[...].reshape(ny * 8, par.shape[2]),
                slots[...],
                precision=HIGHEST,
                preferred_element_type=F32,
            )
            mine = jnp.zeros((8, count), F32)
            for t in range(ny):
                mine = jnp.where(behind == t, chosen[t * 8 : (t + 1) * 8], mine)
            face_par[...] = lax.dot_general(
                mine,
                fault_select[...],
                (((1,), (1,)), ((), ())),
                precision=HIGHEST,
                preferred_element_type=F32,
            )
            moved[...] = jnp.zeros_like(moved)
        for copy in copies:
            copy.wait_recv()
        for g in range(4):
            total = jnp.zeros((group, 4 * slot_count), F32)
            for q in range(4):
                piece = recs[turn, q]
                shift = ((q - g) % 4) * slot_count
                if shift:
                    piece = pltpu.roll(piece, shift, 1)
                total = jnp.where(lane_group == q, piece, total)
            table_in[g * group : (g + 1) * group, :] = total
        nbr_tab[...] += pick(two_parts(table_in[0:table_rows, :]), select[faces:, :])

        def face_flux(f, carry):
            lanes = pl.ds(pl.multiple_of(f * elems, elems), elems)
            at = pl.ds(pl.multiple_of(f * rows, 8), rows)
            accs = [None] * VARS
            for s in range(VARS):
                value = nbr_tab[s * rows : (s + 1) * rows, lanes]
                for i in range(VARS):
                    term = nbr_mats[f, i, s : s + 1, :] * value
                    accs[i] = term if s == 0 else accs[i] + term
            state = []
            for tv, vv in ((0, 6), (3, 7), (5, 8)):
                m_t = own_tab[tv * rows : (tv + 1) * rows, lanes]
                n_t = nbr_tab[tv * rows : (tv + 1) * rows, lanes]
                m_v = own_tab[vv * rows : (vv + 1) * rows, lanes]
                n_v = nbr_tab[vv * rows : (vv + 1) * rows, lanes]
                state.append(0.5 * (m_t + n_t) + 0.5 * (n_v - m_v))
            slip = face_par[0:1, lanes]
            coeff = 0.6 - 0.3 * jnp.minimum(slip / 0.5, 1.0)
            strength = face_par[1:2, lanes] + coeff * jnp.maximum(-state[0], 0.0)
            size = jnp.sqrt(state[1] * state[1] + state[2] * state[2])
            slipping = face_par[2:3, lanes] > 0.5
            ratio = jnp.where(slipping, strength / jnp.maximum(size, strength), 1.0)
            accs[3] = accs[3] + state[1] * (ratio - 1.0)
            accs[5] = accs[5] + state[2] * (ratio - 1.0)
            for i in range(VARS):
                flux[at, i * elems : (i + 1) * elems] += accs[i]
            gain = jnp.sum(size * (1.0 - ratio), axis=0, keepdims=True) / points
            face_par[0:1, lanes] = slip + gain
            moved[0:1, lanes] += gain
            return carry

        lax.fori_loop(0, 4, face_flux, 0)
        if turn == 1:
            per_fault = jnp.dot(
                moved[...], fault_select[...], precision=HIGHEST, preferred_element_type=F32
            )[0:1]
            ways = -(-ny // 8) * 8
            spread = jnp.where(iota_f((ways, count), 0) == ahead, per_fault, 0.0)
            to_slots = lax.dot_general(
                spread,
                slots[...],
                (((1,), (1,)), ((), ())),
                precision=HIGHEST,
                preferred_element_type=F32,
            )
            for t in range(ny):
                ret[t] = jnp.broadcast_to(to_slots[t : t + 1], ret.shape[1:])
            for t in range(1, ny):
                copy = pltpu.make_async_remote_copy(
                    src_ref=ret.at[t],
                    dst_ref=got.at[t],
                    send_sem=ret_send.at[t],
                    recv_sem=ret_recv.at[t],
                    device_id=peer(t),
                    device_id_type=MESH,
                )
                copy.start()
                ret_copies.append(copy)
        lifted = dot_split(lift[...], flux[...])
        for v in range(VARS):
            inc[v] -= lifted[:, v * elems : (v + 1) * elems]
        trace_copies.extend(copies)

    def plastic(values):
        mean = (values[0] + values[1] + values[2]) / 3.0
        dev = [values[v] - mean for v in range(3)]
        total = dev[0] * dev[0] + dev[1] * dev[1] + dev[2] * dev[2]
        shear = values[3] * values[3] + values[4] * values[4] + values[5] * values[5]
        second = jnp.sum(total + 2.0 * shear, axis=0, keepdims=True) / (2.0 * modes)
        equiv = jnp.sqrt(second + 1e-06)
        factor = 1.0 - mask[...].astype(F32) * 0.5 * jnp.maximum(
            1.0 - yield_stress[...] / equiv, 0.0
        )
        return [mean + factor * d for d in dev] + [factor * values[v] for v in range(3, 6)]

    par_copies, ret_copies, trace_copies = [], [], []
    predict(wave, True)
    pl.semaphore_wait(barrier, ny + 1)
    par[0] = jnp.zeros(par.shape[1:], F32)
    par[0, 0:1] = slip0[...]
    par[0, 1:2] = cohesion[...]
    par[0, 2:3] = flag[...].astype(F32)
    for t in range(1, ny):
        copy = pltpu.make_async_remote_copy(
            src_ref=par.at[0],
            dst_ref=par.at[t],
            send_sem=par_send.at[t],
            recv_sem=par_recv.at[t],
            device_id=peer(t),
            device_id_type=MESH,
        )
        copy.start()
        par_copies.append(copy)
    advance(early, 0)
    coarse = cluster[...] == 1
    tried = plastic([wave[v] + inc[v] for v in range(6)])
    for v in range(VARS):
        new = tried[v] if v < 6 else wave[v] + inc[v]
        carried[v] = jnp.where(coarse, inc[v], 0.0)
        mid[v] = jnp.where(coarse, wave[v], new)
    predict(mid, False)
    for v in range(VARS):
        early[v] = jnp.where(coarse, late[v], early[v])
    advance(early, 1)
    done = plastic([(mid[v] + inc[v]) + carried[v] for v in range(6)])
    for v in range(VARS):
        out[v] = done[v] if v < 6 else (mid[v] + inc[v]) + carried[v]
    total = slip0[...] + ret[0, 0:1]
    for t in range(1, ny):
        ret_copies[t - 1].wait_recv()
        total = total + got[t, 0:1]
    slip_out[...] = total
    for copy in par_copies + trace_copies + ret_copies:
        copy.wait_send()


def local(
    nx,
    ny,
    wavefield,
    star_mats,
    flux_own,
    flux_nbr,
    stiffness,
    face_proj,
    lift_mats,
    cluster,
    yield_stress,
    plastic_mask,
    face_source,
    send_faces,
    fault_faces,
    fault_owner,
    fault_slip,
    cohesion,
    slip_flag,
):
    modes, elems = wavefield.shape[1:]
    points = face_proj.shape[1]
    rows = up8(points)
    slot_count = send_faces.shape[1]
    count = fault_faces.shape[1]
    owned = fault_slip.shape[0]
    pad = rows - points
    stiff = jnp.transpose(stiffness, (1, 0, 2)).reshape(modes, 3 * modes)
    stiff_t = jnp.transpose(stiffness, (2, 0, 1)).reshape(modes, 3 * modes)
    proj = jnp.pad(face_proj, ((0, 0), (0, pad), (0, 0))).reshape(4 * rows, modes)
    lift = jnp.pad(jnp.transpose(lift_mats, (1, 0, 2)), ((0, 0), (0, 0), (0, pad)))
    lift = lift.reshape(modes, 4 * rows)
    sends = send_faces[jnp.array([1, 0, 3, 2])].reshape(1, 4 * slot_count)
    group = up8(-(-VARS * rows // 4))
    field = pltpu.VMEM((VARS, modes, elems), F32)
    vmem = pl.BlockSpec(memory_space=pltpu.VMEM)
    out, slip = pl.pallas_call(
        functools.partial(kernel, (nx, ny, points)),
        out_shape=(
            jax.ShapeDtypeStruct(wavefield.shape, F32),
            jax.ShapeDtypeStruct((1, owned), F32),
        ),
        in_specs=[vmem] * 18,
        out_specs=(vmem, vmem),
        scratch_shapes=[field] * 6
        + [
            pltpu.VMEM((3 * modes, VARS * elems), F32),
            pltpu.VMEM((VARS * rows, 4 * elems), F32),
            pltpu.VMEM((VARS * rows, 4 * elems), F32),
            pltpu.VMEM((4 * rows, VARS * elems), F32),
            pltpu.VMEM((4 * elems + 4 * slot_count, 4 * elems), BF16),
            pltpu.VMEM((4 * elems, 4 * slot_count), BF16),
            pltpu.VMEM((4 * elems, count), F32),
            pltpu.VMEM((owned, count), F32),
            pltpu.VMEM((ny, 8, owned), F32),
            pltpu.VMEM((8, 4 * elems), F32),
            pltpu.VMEM((8, 4 * elems), F32),
            pltpu.VMEM((ny, 8, owned), F32),
            pltpu.VMEM((ny, 8, owned), F32),
            pltpu.VMEM((2, 4, group, 4 * slot_count), F32),
            pltpu.VMEM((2, 4, group, 4 * slot_count), F32),
            pltpu.VMEM((4 * group, 4 * slot_count), F32),
            pltpu.SemaphoreType.DMA((ny,)),
            pltpu.SemaphoreType.DMA((ny,)),
            pltpu.SemaphoreType.DMA((ny,)),
            pltpu.SemaphoreType.DMA((ny,)),
            pltpu.SemaphoreType.DMA((2, 4)),
            pltpu.SemaphoreType.DMA((2, 4)),
        ],
        compiler_params=pltpu.CompilerParams(
            collective_id=0, has_side_effects=True, vmem_limit_bytes=48 * 1024 * 1024
        ),
    )(
        wavefield,
        star_mats,
        flux_own,
        flux_nbr,
        stiff,
        stiff_t,
        proj,
        lift,
        cluster.reshape(1, elems),
        yield_stress.reshape(1, elems),
        plastic_mask.reshape(1, elems),
        face_source,
        sends,
        fault_faces,
        fault_owner,
        fault_slip.reshape(1, owned),
        cohesion.reshape(1, owned),
        slip_flag.reshape(1, owned),
    )
    return (out, slip.reshape(owned))


def solution(mesh):
    both = ("gx", "gy")
    return jax.shard_map(
        functools.partial(local, mesh.shape["gx"], mesh.shape["gy"]),
        mesh=mesh,
        in_specs=(
            P(None, None, both),
            P(None, None, None, both),
            P(None, None, None, both),
            P(None, None, None, both),
            P(),
            P(),
            P(),
            P(both),
            P(both),
            P(both),
            P(None, both),
            P(both, None),
            P(both, None),
            P(both, None),
            P(both),
            P(both),
            P(both),
        ),
        out_specs=(P(None, None, both), P(both)),
        check_vma=False,
    )
```

```python
import functools
import math

import jax
import jax.numpy as jnp
from jax import lax
from jax.experimental import pallas as pl
from jax.experimental.pallas import tpu as pltpu
from jax.sharding import PartitionSpec as P

VARS = 9
ORDER = 6
HIGHEST = lax.Precision.HIGHEST
F32 = jnp.float32
BF16 = jnp.bfloat16


def up8(n):
    return -(-n // 8) * 8


def iota_f(shape, axis):
    return lax.broadcasted_iota(jnp.int32, shape, axis).astype(F32)


def dot(a, b):
    return jnp.dot(a, b, preferred_element_type=F32)


def low_part(x):
    return x - x.astype(BF16).astype(F32)


def two_parts(x):
    return jnp.concatenate([x, low_part(x)], axis=0).astype(BF16)


def left_parts(mat):
    return jnp.concatenate([mat, low_part(mat), mat], axis=1).astype(BF16)


def right_parts(data):
    return jnp.concatenate([data, data, low_part(data)], axis=0).astype(BF16)


def pick(parts, select):
    rows = parts.shape[0] // 2
    both = dot(parts, select)
    return both[:rows] + both[rows:]


def kernel(
    cfg,
    wave_hbm,
    star_hbm,
    own_hbm,
    nbr_hbm,
    stiff_hbm,
    proj_hbm,
    lift_hbm,
    cluster,
    yield_stress,
    mask,
    source,
    sends,
    faults,
    owners,
    slip0,
    cohesion,
    flag,
    out,
    slip_out,
    wave,
    star,
    own_mats,
    nbr_mats,
    stiff_in,
    proj_in,
    lift_in,
    deriv,
    early,
    late,
    mid,
    inc,
    carried,
    mix,
    own_tab,
    nbr_tab,
    flux,
    faces_in,
    stiff,
    stiff_t,
    proj,
    lift,
    select,
    send_select,
    fault_select,
    slots,
    par,
    face_par,
    moved,
    ret,
    got,
    packs,
    recs,
    table_in,
    par_send,
    par_recv,
    ret_send,
    ret_recv,
    tr_send,
    tr_recv,
    in_sems,
):
    nx, ny, points = cfg
    modes, elems = wave.shape[1:]
    rows = up8(points)
    faces = 4 * elems
    slot_count = sends.shape[1]
    group = packs.shape[2]
    table_rows = VARS * rows
    cap = slip0.shape[1] // ny
    ix, iy = lax.axis_index("gx"), lax.axis_index("gy")
    x_up = (lax.rem(ix + 1, nx), iy)
    x_down = (lax.rem(ix + nx - 1, nx), iy)
    y_up = (ix, lax.rem(iy + 1, ny))
    y_down = (ix, lax.rem(iy + ny - 1, ny))
    MESH = pl.DeviceIdType.MESH

    def peer(step):
        return (ix, lax.rem(iy + step, ny))

    barrier = pltpu.get_barrier_semaphore()
    for target in [x_up, x_down] + [peer(t) for t in range(1, ny)]:
        pl.semaphore_signal(barrier, inc=1, device_id=target, device_id_type=MESH)

    fetches = {}
    for k, (src, dst) in enumerate(
        (
            (stiff_hbm, stiff_in),
            (proj_hbm, proj_in),
            (lift_hbm, lift_in),
            (wave_hbm, wave),
            (star_hbm, star),
            (own_hbm, own_mats),
            (nbr_hbm, nbr_mats),
        )
    ):
        fetches[k] = pltpu.make_async_copy(src, dst, in_sems.at[k])
        fetches[k].start()
    me = iy.astype(F32)
    table_size = select.shape[0]
    for f in range(4):
        want = source[f : f + 1, :].astype(F32)
        hit = iota_f((table_size, elems), 0) == want
        select[:, f * elems : (f + 1) * elems] = jnp.where(hit, 1.0, 0.0).astype(BF16)
    row = jnp.concatenate([sends[d : d + 1, :] for d in (1, 0, 3, 2)], axis=1)
    hit = iota_f((faces, 4 * slot_count), 0) == row.astype(F32)
    send_select[...] = jnp.where(hit, 1.0, 0.0).astype(BF16)
    count = faults.shape[1]
    hit = iota_f((faces, count), 0) == faults[...].astype(F32)
    fault_select[...] = jnp.where(hit, 1.0, 0.0)
    owner_row = owners[...].astype(F32)
    r, c = iota_f((count, count), 0), iota_f((count, count), 1)
    owner_col = jnp.sum(jnp.where(r == c, owner_row, 0.0), axis=1, keepdims=True)
    same = jnp.where((owner_col == owner_row) & (r < c), 1.0, 0.0)
    rank = jnp.sum(same, axis=0, keepdims=True)
    slot_row = me * cap + rank
    slots[...] = jnp.where(iota_f((slip0.shape[1], count), 0) == slot_row, 1.0, 0.0)
    away = owner_row - me
    ahead = jnp.where(away < 0, away + ny, away)
    behind = jnp.where(away > 0, ny - away, -away)

    for k in range(3):
        fetches[k].wait()
    stiff[...] = left_parts(stiff_in[...].reshape(3 * modes, modes))
    turned = [jnp.transpose(stiff_in[d]) for d in range(3)]
    stiff_t[...] = left_parts(jnp.concatenate(turned, axis=0))
    for source_in, kept in ((proj_in, proj), (lift_in, lift)):
        faces_in[...] = jnp.zeros_like(faces_in)
        for f in range(4):
            faces_in[f * rows : f * rows + points, :] = source_in[:, f, :]
        if kept is proj:
            kept[...] = left_parts(faces_in[...])
        else:
            kept[...] = left_parts(jnp.transpose(faces_in[...]))

    def flat(field):
        return right_parts(jnp.concatenate([field[v] for v in range(VARS)], axis=1))

    def star_sum(first):
        accs = [None] * 3
        for d in range(3):
            for s in range(VARS):
                value = mix[d * modes : (d + 1) * modes, s * elems : (s + 1) * elems]
                for k in range(3):
                    term = star[first + k, s, d : d + 1, :] * value
                    accs[k] = term if accs[k] is None else accs[k] + term
        return accs

    def face_sum(mats, table, first, f):
        accs = [None] * 3
        for s in range(VARS):
            value = table[s * rows : (s + 1) * rows, f * elems : (f + 1) * elems]
            for k in range(3):
                term = mats[first + k, s, f : f + 1, :] * value
                accs[k] = term if s == 0 else accs[k] + term
        return accs

    def predict(src, with_late):
        for v in range(VARS):
            deriv[v] = src[v]
            early[v] = src[v]
            if with_late:
                late[v] = src[v]

        def one_power(power, carry):
            scale_early = jnp.float32(0.0)
            scale_late = jnp.float32(0.0)
            for p in range(2, ORDER + 1):
                scale_early = jnp.where(power == p, 1.0 / math.factorial(p), scale_early)
                scale_late = jnp.where(
                    power == p, (2.0**p - 1.0) / math.factorial(p), scale_late
                )
            mix[...] = dot(stiff[...], flat(deriv))

            def some_vars(third, inner):
                accs = star_sum(third * 3)
                for k in range(3):
                    v = third * 3 + k
                    step = -accs[k]
                    deriv[v] = step
                    early[v] += step * scale_early
                    if with_late:
                        late[v] += step * scale_late
                return inner

            return lax.fori_loop(0, 3, some_vars, carry)

        lax.fori_loop(2, ORDER + 1, one_power, 0)

    def advance(field, turn):
        held = flat(field)
        traces = dot(proj[...], held)
        for v in range(VARS):
            for f in range(4):
                own_tab[v * rows : (v + 1) * rows, f * elems : (f + 1) * elems] = traces[
                    f * rows : (f + 1) * rows, v * elems : (v + 1) * elems
                ]
        own_parts = two_parts(own_tab[...])
        table_in[table_rows:, :] = jnp.zeros((4 * group - table_rows, 4 * slot_count), F32)
        table_in[0:table_rows, :] = pick(own_parts, send_select[...])
        lane_group = lax.broadcasted_iota(jnp.int32, (group, 4 * slot_count), 1) // slot_count
        copies = []
        for q, target in enumerate([x_up, x_down, y_up, y_down]):
            packed = jnp.zeros((group, 4 * slot_count), F32)
            for g in range(4):
                piece = table_in[g * group : (g + 1) * group, :]
                shift = ((g - q) % 4) * slot_count
                if shift:
                    piece = pltpu.roll(piece, shift, 1)
                packed = jnp.where(lane_group == g, piece, packed)
            packs[turn, q] = packed
            copy = pltpu.make_async_remote_copy(
                src_ref=packs.at[turn, q],
                dst_ref=recs.at[turn, q],
                send_sem=tr_send.at[turn, q],
                recv_sem=tr_recv.at[turn, q],
                device_id=target,
                device_id_type=MESH,
            )
            copy.start()
            copies.append(copy)

        mix[...] = dot(stiff_t[...], held)
        nbr_tab[...] = pick(own_parts, select[0:faces, :])

        def own_side(third, carry):
            first = third * 3
            accs = star_sum(first)
            for k in range(3):
                inc[first + k] = accs[k]
            for f in range(4):
                accs = face_sum(own_mats, own_tab, first, f)
                for k in range(3):
                    lanes = pl.ds(pl.multiple_of((first + k) * elems, elems), elems)
                    flux[f * rows : (f + 1) * rows, lanes] = accs[k]
            return carry

        if turn == 0:
            fetches[5].wait()
            fetches[6].wait()
        lax.fori_loop(0, 3, own_side, 0)
        if turn == 0:
            for copy in par_copies:
                copy.wait_recv()
            chosen = jnp.dot(
                par[...].reshape(ny * 8, par.shape[2]),
                slots[...],
                precision=HIGHEST,
                preferred_element_type=F32,
            )
            mine = jnp.zeros((8, count), F32)
            for t in range(ny):
                mine = jnp.where(behind == t, chosen[t * 8 : (t + 1) * 8], mine)
            face_par[...] = lax.dot_general(
                mine,
                fault_select[...],
                (((1,), (1,)), ((), ())),
                precision=HIGHEST,
                preferred_element_type=F32,
            )
            moved[...] = jnp.zeros_like(moved)
        for copy in copies:
            copy.wait_recv()
        for g in range(4):
            total = jnp.zeros((group, 4 * slot_count), F32)
            for q in range(4):
                piece = recs[turn, q]
                shift = ((q - g) % 4) * slot_count
                if shift:
                    piece = pltpu.roll(piece, shift, 1)
                total = jnp.where(lane_group == q, piece, total)
            table_in[g * group : (g + 1) * group, :] = total
        nbr_tab[...] += pick(two_parts(table_in[0:table_rows, :]), select[faces:, :])

        def nbr_side(third, carry):
            first = third * 3
            for f in range(4):
                accs = face_sum(nbr_mats, nbr_tab, first, f)
                for k in range(3):
                    lanes = pl.ds(pl.multiple_of((first + k) * elems, elems), elems)
                    flux[f * rows : (f + 1) * rows, lanes] += accs[k]
            return carry

        lax.fori_loop(0, 3, nbr_side, 0)

        def fault_flux(f, carry):
            lanes = pl.ds(pl.multiple_of(f * elems, elems), elems)
            at = pl.ds(pl.multiple_of(f * rows, 8), rows)
            state = []
            for tv, vv in ((0, 6), (3, 7), (5, 8)):
                m_t = own_tab[tv * rows : (tv + 1) * rows, lanes]
                n_t = nbr_tab[tv * rows : (tv + 1) * rows, lanes]
                m_v = own_tab[vv * rows : (vv + 1) * rows, lanes]
                n_v = nbr_tab[vv * rows : (vv + 1) * rows, lanes]
                state.append(0.5 * (m_t + n_t) + 0.5 * (n_v - m_v))
            slip = face_par[0:1, lanes]
            coeff = 0.6 - 0.3 * jnp.minimum(slip / 0.5, 1.0)
            strength = face_par[1:2, lanes] + coeff * jnp.maximum(-state[0], 0.0)
            size = jnp.sqrt(state[1] * state[1] + state[2] * state[2])
            slipping = face_par[2:3, lanes] > 0.5
            ratio = jnp.where(slipping, strength / jnp.maximum(size, strength), 1.0)
            flux[at, 3 * elems : 4 * elems] += state[1] * (ratio - 1.0)
            flux[at, 5 * elems : 6 * elems] += state[2] * (ratio - 1.0)
            gain = jnp.sum(size * (1.0 - ratio), axis=0, keepdims=True) / points
            face_par[0:1, lanes] = slip + gain
            moved[0:1, lanes] += gain
            return carry

        lax.fori_loop(0, 4, fault_flux, 0)
        if turn == 1:
            per_fault = jnp.dot(
                moved[...], fault_select[...], precision=HIGHEST, preferred_element_type=F32
            )[0:1]
            ways = -(-ny // 8) * 8
            spread = jnp.where(iota_f((ways, count), 0) == ahead, per_fault, 0.0)
            to_slots = lax.dot_general(
                spread,
                slots[...],
                (((1,), (1,)), ((), ())),
                precision=HIGHEST,
                preferred_element_type=F32,
            )
            for t in range(ny):
                ret[t] = jnp.broadcast_to(to_slots[t : t + 1], ret.shape[1:])
            for t in range(1, ny):
                copy = pltpu.make_async_remote_copy(
                    src_ref=ret.at[t],
                    dst_ref=got.at[t],
                    send_sem=ret_send.at[t],
                    recv_sem=ret_recv.at[t],
                    device_id=peer(t),
                    device_id_type=MESH,
                )
                copy.start()
                ret_copies.append(copy)
        lifted = dot(lift[...], right_parts(flux[...]))
        for v in range(VARS):
            inc[v] -= lifted[:, v * elems : (v + 1) * elems]
        trace_copies.extend(copies)

    def plastic(values):
        mean = (values[0] + values[1] + values[2]) / 3.0
        dev = [values[v] - mean for v in range(3)]
        total = dev[0] * dev[0] + dev[1] * dev[1] + dev[2] * dev[2]
        shear = values[3] * values[3] + values[4] * values[4] + values[5] * values[5]
        second = jnp.sum(total + 2.0 * shear, axis=0, keepdims=True) / (2.0 * modes)
        equiv = jnp.sqrt(second + 1e-06)
        factor = 1.0 - mask[...].astype(F32) * 0.5 * jnp.maximum(
            1.0 - yield_stress[...] / equiv, 0.0
        )
        return [mean + factor * d for d in dev] + [factor * values[v] for v in range(3, 6)]

    par_copies, ret_copies, trace_copies = [], [], []
    fetches[3].wait()
    fetches[4].wait()
    predict(wave, True)
    pl.semaphore_wait(barrier, ny + 1)
    par[0] = jnp.zeros(par.shape[1:], F32)
    par[0, 0:1] = slip0[...]
    par[0, 1:2] = cohesion[...]
    par[0, 2:3] = flag[...].astype(F32)
    for t in range(1, ny):
        copy = pltpu.make_async_remote_copy(
            src_ref=par.at[0],
            dst_ref=par.at[t],
            send_sem=par_send.at[t],
            recv_sem=par_recv.at[t],
            device_id=peer(t),
            device_id_type=MESH,
        )
        copy.start()
        par_copies.append(copy)
    advance(early, 0)
    coarse = cluster[...] == 1
    tried = plastic([wave[v] + inc[v] for v in range(6)])
    for v in range(VARS):
        new = tried[v] if v < 6 else wave[v] + inc[v]
        carried[v] = jnp.where(coarse, inc[v], 0.0)
        mid[v] = jnp.where(coarse, wave[v], new)
    predict(mid, False)
    for v in range(VARS):
        early[v] = jnp.where(coarse, late[v], early[v])
    advance(early, 1)
    done = plastic([(mid[v] + inc[v]) + carried[v] for v in range(6)])
    for v in range(VARS):
        out[v] = done[v] if v < 6 else (mid[v] + inc[v]) + carried[v]
    total = slip0[...] + ret[0, 0:1]
    for t in range(1, ny):
        ret_copies[t - 1].wait_recv()
        total = total + got[t, 0:1]
    slip_out[...] = total
    for copy in par_copies + trace_copies + ret_copies:
        copy.wait_send()


def local(
    nx,
    ny,
    wavefield,
    star_mats,
    flux_own,
    flux_nbr,
    stiffness,
    face_proj,
    lift_mats,
    cluster,
    yield_stress,
    plastic_mask,
    face_source,
    send_faces,
    fault_faces,
    fault_owner,
    fault_slip,
    cohesion,
    slip_flag,
):
    modes, elems = wavefield.shape[1:]
    points = face_proj.shape[1]
    rows = up8(points)
    slot_count = send_faces.shape[1]
    count = fault_faces.shape[1]
    owned = fault_slip.shape[0]
    group = up8(-(-VARS * rows // 4))
    fetched = (
        wavefield,
        jnp.transpose(star_mats, (1, 2, 0, 3)),
        jnp.transpose(flux_own, (1, 2, 0, 3)),
        jnp.transpose(flux_nbr, (1, 2, 0, 3)),
        stiffness,
        jnp.transpose(face_proj, (1, 0, 2)),
        jnp.transpose(lift_mats, (2, 0, 1)),
    )
    field = pltpu.VMEM((VARS, modes, elems), F32)
    vmem = pl.BlockSpec(memory_space=pltpu.VMEM)
    out, slip = pl.pallas_call(
        functools.partial(kernel, (nx, ny, points)),
        out_shape=(
            jax.ShapeDtypeStruct(wavefield.shape, F32),
            jax.ShapeDtypeStruct((1, owned), F32),
        ),
        in_specs=[pl.BlockSpec(memory_space=pl.ANY)] * 7 + [vmem] * 10,
        out_specs=(vmem, vmem),
        scratch_shapes=[pltpu.VMEM(x.shape, F32) for x in fetched]
        + [field] * 6
        + [
            pltpu.VMEM((3 * modes, VARS * elems), F32),
            pltpu.VMEM((VARS * rows, 4 * elems), F32),
            pltpu.VMEM((VARS * rows, 4 * elems), F32),
            pltpu.VMEM((4 * rows, VARS * elems), F32),
            pltpu.VMEM((4 * rows, modes), F32),
            pltpu.VMEM((3 * modes, 3 * modes), BF16),
            pltpu.VMEM((3 * modes, 3 * modes), BF16),
            pltpu.VMEM((4 * rows, 3 * modes), BF16),
            pltpu.VMEM((modes, 12 * rows), BF16),
            pltpu.VMEM((4 * elems + 4 * slot_count, 4 * elems), BF16),
            pltpu.VMEM((4 * elems, 4 * slot_count), BF16),
            pltpu.VMEM((4 * elems, count), F32),
            pltpu.VMEM((owned, count), F32),
            pltpu.VMEM((ny, 8, owned), F32),
            pltpu.VMEM((8, 4 * elems), F32),
            pltpu.VMEM((8, 4 * elems), F32),
            pltpu.VMEM((ny, 8, owned), F32),
            pltpu.VMEM((ny, 8, owned), F32),
            pltpu.VMEM((2, 4, group, 4 * slot_count), F32),
            pltpu.VMEM((2, 4, group, 4 * slot_count), F32),
            pltpu.VMEM((4 * group, 4 * slot_count), F32),
            pltpu.SemaphoreType.DMA((ny,)),
            pltpu.SemaphoreType.DMA((ny,)),
            pltpu.SemaphoreType.DMA((ny,)),
            pltpu.SemaphoreType.DMA((ny,)),
            pltpu.SemaphoreType.DMA((2, 4)),
            pltpu.SemaphoreType.DMA((2, 4)),
            pltpu.SemaphoreType.DMA((len(fetched),)),
        ],
        compiler_params=pltpu.CompilerParams(
            collective_id=0, has_side_effects=True, vmem_limit_bytes=60 * 1024 * 1024
        ),
    )(
        *fetched,
        cluster.reshape(1, elems),
        yield_stress.reshape(1, elems),
        plastic_mask.reshape(1, elems),
        face_source,
        send_faces,
        fault_faces,
        fault_owner.reshape(1, count),
        fault_slip.reshape(1, owned),
        cohesion.reshape(1, owned),
        slip_flag.reshape(1, owned),
    )
    return (out, slip.reshape(owned))


def solution(mesh):
    both = ("gx", "gy")
    return jax.shard_map(
        functools.partial(local, mesh.shape["gx"], mesh.shape["gy"]),
        mesh=mesh,
        in_specs=(
            P(None, None, both),
            P(None, None, None, both),
            P(None, None, None, both),
            P(None, None, None, both),
            P(),
            P(),
            P(),
            P(both),
            P(both),
            P(both),
            P(None, both),
            P(both, None),
            P(both, None),
            P(both, None),
            P(both),
            P(both),
            P(both),
        ),
        out_specs=(P(None, None, both), P(both)),
        check_vma=False,
    )
```

```python
import functools
import math

import jax
import jax.numpy as jnp
from jax import lax
from jax.experimental import pallas as pl
from jax.experimental.pallas import tpu as pltpu
from jax.sharding import PartitionSpec as P

VARS = 9
ORDER = 6
HIGHEST = lax.Precision.HIGHEST
F32 = jnp.float32
BF16 = jnp.bfloat16


def up8(n):
    return -(-n // 8) * 8


def iota_f(shape, axis):
    return lax.broadcasted_iota(jnp.int32, shape, axis).astype(F32)


def dot(a, b):
    return jnp.dot(a, b, preferred_element_type=F32)


def low_part(x):
    return x - x.astype(BF16).astype(F32)


def two_parts(x):
    return jnp.concatenate([x, low_part(x)], axis=0).astype(BF16)


def left_parts(mat):
    return jnp.concatenate([mat, low_part(mat), mat], axis=1).astype(BF16)


def right_parts(data):
    return jnp.concatenate([data, data, low_part(data)], axis=0).astype(BF16)


def pick(parts, select):
    rows = parts.shape[0] // 2
    both = dot(parts, select)
    return both[:rows] + both[rows:]


def kernel(
    cfg,
    wave_hbm,
    star_hbm,
    own_hbm,
    nbr_hbm,
    stiff_hbm,
    proj_hbm,
    lift_hbm,
    cluster,
    yield_stress,
    mask,
    source,
    sends,
    faults,
    owners,
    slip0,
    cohesion,
    flag,
    out,
    slip_out,
    wave,
    star,
    own_mats,
    nbr_mats,
    stiff_in,
    proj_in,
    lift_in,
    deriv,
    early,
    late,
    mid,
    inc,
    carried,
    mix,
    own_tab,
    nbr_tab,
    flux,
    faces_in,
    stiff,
    stiff_t,
    proj,
    lift,
    select,
    send_select,
    fault_select,
    slots,
    par,
    face_par,
    moved,
    ret,
    got,
    packs,
    recs,
    table_in,
    par_send,
    par_recv,
    ret_send,
    ret_recv,
    tr_send,
    tr_recv,
    in_sems,
):
    nx, ny, points = cfg
    modes, elems = wave.shape[1:]
    rows = up8(points)
    faces = 4 * elems
    slot_count = sends.shape[1]
    group = packs.shape[2]
    table_rows = VARS * rows
    cap = slip0.shape[1] // ny
    ix, iy = lax.axis_index("gx"), lax.axis_index("gy")
    x_up = (lax.rem(ix + 1, nx), iy)
    x_down = (lax.rem(ix + nx - 1, nx), iy)
    y_up = (ix, lax.rem(iy + 1, ny))
    y_down = (ix, lax.rem(iy + ny - 1, ny))
    MESH = pl.DeviceIdType.MESH

    def peer(step):
        return (ix, lax.rem(iy + step, ny))

    barrier = pltpu.get_barrier_semaphore()
    for target in [x_up, x_down] + [peer(t) for t in range(1, ny)]:
        pl.semaphore_signal(barrier, inc=1, device_id=target, device_id_type=MESH)

    fetches = {}
    for k, (src, dst) in enumerate(
        (
            (stiff_hbm, stiff_in),
            (proj_hbm, proj_in),
            (lift_hbm, lift_in),
            (wave_hbm, wave),
            (star_hbm, star),
            (own_hbm, own_mats),
            (nbr_hbm, nbr_mats),
        )
    ):
        fetches[k] = pltpu.make_async_copy(src, dst, in_sems.at[k])
        fetches[k].start()
    me = iy.astype(F32)
    row = jnp.concatenate([sends[d : d + 1, :] for d in (1, 0, 3, 2)], axis=1)
    hit = iota_f((faces, 4 * slot_count), 0) == row.astype(F32)
    send_select[...] = jnp.where(hit, 1.0, 0.0).astype(BF16)
    count = faults.shape[1]
    hit = iota_f((faces, count), 0) == faults[...].astype(F32)
    fault_select[...] = jnp.where(hit, 1.0, 0.0)
    owner_row = owners[...].astype(F32)
    r, c = iota_f((count, count), 0), iota_f((count, count), 1)
    owner_col = jnp.sum(jnp.where(r == c, owner_row, 0.0), axis=1, keepdims=True)
    same = jnp.where((owner_col == owner_row) & (r < c), 1.0, 0.0)
    rank = jnp.sum(same, axis=0, keepdims=True)
    slot_row = me * cap + rank
    slots[...] = jnp.where(iota_f((slip0.shape[1], count), 0) == slot_row, 1.0, 0.0)
    away = owner_row - me
    ahead = jnp.where(away < 0, away + ny, away)
    behind = jnp.where(away > 0, ny - away, -away)

    for k in range(3):
        fetches[k].wait()
    stiff[...] = left_parts(stiff_in[...].reshape(3 * modes, modes))
    turned = [jnp.transpose(stiff_in[d]) for d in range(3)]
    stiff_t[...] = left_parts(jnp.concatenate(turned, axis=0))
    for source_in, kept in ((proj_in, proj), (lift_in, lift)):
        faces_in[...] = jnp.zeros_like(faces_in)
        for f in range(4):
            faces_in[f * rows : f * rows + points, :] = source_in[:, f, :]
        if kept is proj:
            kept[...] = left_parts(faces_in[...])
        else:
            kept[...] = left_parts(jnp.transpose(faces_in[...]))

    def flat(field):
        return right_parts(jnp.concatenate([field[v] for v in range(VARS)], axis=1))

    def star_sum(first):
        accs = [None] * 3
        for d in range(3):
            for s in range(VARS):
                value = mix[d * modes : (d + 1) * modes, s * elems : (s + 1) * elems]
                for k in range(3):
                    term = star[first + k, s, d : d + 1, :] * value
                    accs[k] = term if accs[k] is None else accs[k] + term
        return accs

    def face_sum(mats, table, first, f):
        accs = [None] * 3
        for s in range(VARS):
            value = table[s * rows : (s + 1) * rows, f * elems : (f + 1) * elems]
            for k in range(3):
                term = mats[first + k, s, f : f + 1, :] * value
                accs[k] = term if s == 0 else accs[k] + term
        return accs

    def predict(src, with_late):
        for v in range(VARS):
            deriv[v] = src[v]
            early[v] = src[v]
            if with_late:
                late[v] = src[v]

        def one_power(power, carry):
            scale_early = jnp.float32(0.0)
            scale_late = jnp.float32(0.0)
            for p in range(2, ORDER + 1):
                scale_early = jnp.where(power == p, 1.0 / math.factorial(p), scale_early)
                scale_late = jnp.where(
                    power == p, (2.0**p - 1.0) / math.factorial(p), scale_late
                )
            mix[...] = dot(stiff[...], flat(deriv))

            def some_vars(third, inner):
                accs = star_sum(third * 3)
                for k in range(3):
                    v = third * 3 + k
                    step = -accs[k]
                    deriv[v] = step
                    early[v] += step * scale_early
                    if with_late:
                        late[v] += step * scale_late
                return inner

            return lax.fori_loop(0, 3, some_vars, carry)

        lax.fori_loop(2, ORDER + 1, one_power, 0)

    def advance(field, turn):
        held = flat(field)
        traces = dot(proj[...], held)
        for v in range(VARS):
            for f in range(4):
                own_tab[v * rows : (v + 1) * rows, f * elems : (f + 1) * elems] = traces[
                    f * rows : (f + 1) * rows, v * elems : (v + 1) * elems
                ]
        own_parts = two_parts(own_tab[...])
        table_in[table_rows:, :] = jnp.zeros((4 * group - table_rows, 4 * slot_count), F32)
        table_in[0:table_rows, :] = pick(own_parts, send_select[...])
        lane_group = lax.broadcasted_iota(jnp.int32, (group, 4 * slot_count), 1) // slot_count
        copies = []
        for q, target in enumerate([x_up, x_down, y_up, y_down]):
            packed = jnp.zeros((group, 4 * slot_count), F32)
            for g in range(4):
                piece = table_in[g * group : (g + 1) * group, :]
                shift = ((g - q) % 4) * slot_count
                if shift:
                    piece = pltpu.roll(piece, shift, 1)
                packed = jnp.where(lane_group == g, piece, packed)
            packs[turn, q] = packed
            copy = pltpu.make_async_remote_copy(
                src_ref=packs.at[turn, q],
                dst_ref=recs.at[turn, q],
                send_sem=tr_send.at[turn, q],
                recv_sem=tr_recv.at[turn, q],
                device_id=target,
                device_id_type=MESH,
            )
            copy.start()
            copies.append(copy)

        if turn == 0:
            table_size = select.shape[0]
            for f in range(4):
                want = source[f : f + 1, :].astype(F32)
                hit = iota_f((table_size, elems), 0) == want
                select[:, f * elems : (f + 1) * elems] = jnp.where(hit, 1.0, 0.0).astype(BF16)
        mix[...] = dot(stiff_t[...], held)
        nbr_tab[...] = pick(own_parts, select[0:faces, :])

        def own_side(third, carry):
            first = third * 3
            accs = star_sum(first)
            for k in range(3):
                inc[first + k] = accs[k]
            for f in range(4):
                accs = face_sum(own_mats, own_tab, first, f)
                for k in range(3):
                    lanes = pl.ds(pl.multiple_of((first + k) * elems, elems), elems)
                    flux[f * rows : (f + 1) * rows, lanes] = accs[k]
            return carry

        if turn == 0:
            fetches[5].wait()
            fetches[6].wait()
        lax.fori_loop(0, 3, own_side, 0)
        if turn == 0:
            for copy in par_copies:
                copy.wait_recv()
            chosen = jnp.dot(
                par[...].reshape(ny * 8, par.shape[2]),
                slots[...],
                precision=HIGHEST,
                preferred_element_type=F32,
            )
            mine = jnp.zeros((8, count), F32)
            for t in range(ny):
                mine = jnp.where(behind == t, chosen[t * 8 : (t + 1) * 8], mine)
            face_par[...] = lax.dot_general(
                mine,
                fault_select[...],
                (((1,), (1,)), ((), ())),
                precision=HIGHEST,
                preferred_element_type=F32,
            )
            moved[...] = jnp.zeros_like(moved)
        for copy in copies:
            copy.wait_recv()
        for g in range(4):
            total = jnp.zeros((group, 4 * slot_count), F32)
            for q in range(4):
                piece = recs[turn, q]
                shift = ((q - g) % 4) * slot_count
                if shift:
                    piece = pltpu.roll(piece, shift, 1)
                total = jnp.where(lane_group == q, piece, total)
            table_in[g * group : (g + 1) * group, :] = total
        nbr_tab[...] += pick(two_parts(table_in[0:table_rows, :]), select[faces:, :])

        def nbr_side(third, carry):
            first = third * 3
            for f in range(4):
                accs = face_sum(nbr_mats, nbr_tab, first, f)
                for k in range(3):
                    lanes = pl.ds(pl.multiple_of((first + k) * elems, elems), elems)
                    flux[f * rows : (f + 1) * rows, lanes] += accs[k]
            return carry

        lax.fori_loop(0, 3, nbr_side, 0)

        def fault_flux(f, carry):
            lanes = pl.ds(pl.multiple_of(f * elems, elems), elems)
            at = pl.ds(pl.multiple_of(f * rows, 8), rows)
            state = []
            for tv, vv in ((0, 6), (3, 7), (5, 8)):
                m_t = own_tab[tv * rows : (tv + 1) * rows, lanes]
                n_t = nbr_tab[tv * rows : (tv + 1) * rows, lanes]
                m_v = own_tab[vv * rows : (vv + 1) * rows, lanes]
                n_v = nbr_tab[vv * rows : (vv + 1) * rows, lanes]
                state.append(0.5 * (m_t + n_t) + 0.5 * (n_v - m_v))
            slip = face_par[0:1, lanes]
            coeff = 0.6 - 0.3 * jnp.minimum(slip / 0.5, 1.0)
            strength = face_par[1:2, lanes] + coeff * jnp.maximum(-state[0], 0.0)
            size = jnp.sqrt(state[1] * state[1] + state[2] * state[2])
            slipping = face_par[2:3, lanes] > 0.5
            ratio = jnp.where(slipping, strength / jnp.maximum(size, strength), 1.0)
            flux[at, 3 * elems : 4 * elems] += state[1] * (ratio - 1.0)
            flux[at, 5 * elems : 6 * elems] += state[2] * (ratio - 1.0)
            gain = jnp.sum(size * (1.0 - ratio), axis=0, keepdims=True) / points
            face_par[0:1, lanes] = slip + gain
            moved[0:1, lanes] += gain
            return carry

        lax.fori_loop(0, 4, fault_flux, 0)
        if turn == 1:
            per_fault = jnp.dot(
                moved[...], fault_select[...], precision=HIGHEST, preferred_element_type=F32
            )[0:1]
            ways = -(-ny // 8) * 8
            spread = jnp.where(iota_f((ways, count), 0) == ahead, per_fault, 0.0)
            to_slots = lax.dot_general(
                spread,
                slots[...],
                (((1,), (1,)), ((), ())),
                precision=HIGHEST,
                preferred_element_type=F32,
            )
            for t in range(ny):
                ret[t] = jnp.broadcast_to(to_slots[t : t + 1], ret.shape[1:])
            for t in range(1, ny):
                copy = pltpu.make_async_remote_copy(
                    src_ref=ret.at[t],
                    dst_ref=got.at[t],
                    send_sem=ret_send.at[t],
                    recv_sem=ret_recv.at[t],
                    device_id=peer(t),
                    device_id_type=MESH,
                )
                copy.start()
                ret_copies.append(copy)
        lifted = dot(lift[...], right_parts(flux[...]))
        for v in range(VARS):
            inc[v] -= lifted[:, v * elems : (v + 1) * elems]
        trace_copies.extend(copies)

    def plastic(values):
        mean = (values[0] + values[1] + values[2]) / 3.0
        dev = [values[v] - mean for v in range(3)]
        total = dev[0] * dev[0] + dev[1] * dev[1] + dev[2] * dev[2]
        shear = values[3] * values[3] + values[4] * values[4] + values[5] * values[5]
        second = jnp.sum(total + 2.0 * shear, axis=0, keepdims=True) / (2.0 * modes)
        equiv = jnp.sqrt(second + 1e-06)
        factor = 1.0 - mask[...].astype(F32) * 0.5 * jnp.maximum(
            1.0 - yield_stress[...] / equiv, 0.0
        )
        return [mean + factor * d for d in dev] + [factor * values[v] for v in range(3, 6)]

    par_copies, ret_copies, trace_copies = [], [], []
    fetches[3].wait()
    fetches[4].wait()
    predict(wave, True)
    pl.semaphore_wait(barrier, ny + 1)
    par[0] = jnp.zeros(par.shape[1:], F32)
    par[0, 0:1] = slip0[...]
    par[0, 1:2] = cohesion[...]
    par[0, 2:3] = flag[...].astype(F32)
    for t in range(1, ny):
        copy = pltpu.make_async_remote_copy(
            src_ref=par.at[0],
            dst_ref=par.at[t],
            send_sem=par_send.at[t],
            recv_sem=par_recv.at[t],
            device_id=peer(t),
            device_id_type=MESH,
        )
        copy.start()
        par_copies.append(copy)
    advance(early, 0)
    coarse = cluster[...] == 1
    tried = plastic([wave[v] + inc[v] for v in range(6)])
    for v in range(VARS):
        new = tried[v] if v < 6 else wave[v] + inc[v]
        carried[v] = jnp.where(coarse, inc[v], 0.0)
        mid[v] = jnp.where(coarse, wave[v], new)
    predict(mid, False)
    for v in range(VARS):
        early[v] = jnp.where(coarse, late[v], early[v])
    advance(early, 1)
    done = plastic([(mid[v] + inc[v]) + carried[v] for v in range(6)])
    for v in range(VARS):
        out[v] = done[v] if v < 6 else (mid[v] + inc[v]) + carried[v]
    total = slip0[...] + ret[0, 0:1]
    for t in range(1, ny):
        ret_copies[t - 1].wait_recv()
        total = total + got[t, 0:1]
    slip_out[...] = total
    for copy in par_copies + trace_copies + ret_copies:
        copy.wait_send()


def local(
    nx,
    ny,
    wavefield,
    star_mats,
    flux_own,
    flux_nbr,
    stiffness,
    face_proj,
    lift_mats,
    cluster,
    yield_stress,
    plastic_mask,
    face_source,
    send_faces,
    fault_faces,
    fault_owner,
    fault_slip,
    cohesion,
    slip_flag,
):
    modes, elems = wavefield.shape[1:]
    points = face_proj.shape[1]
    rows = up8(points)
    slot_count = send_faces.shape[1]
    count = fault_faces.shape[1]
    owned = fault_slip.shape[0]
    group = up8(-(-VARS * rows // 4))
    fetched = (
        wavefield,
        jnp.transpose(star_mats, (1, 2, 0, 3)),
        jnp.transpose(flux_own, (1, 2, 0, 3)),
        jnp.transpose(flux_nbr, (1, 2, 0, 3)),
        stiffness,
        jnp.transpose(face_proj, (1, 0, 2)),
        jnp.transpose(lift_mats, (2, 0, 1)),
    )
    field = pltpu.VMEM((VARS, modes, elems), F32)
    vmem = pl.BlockSpec(memory_space=pltpu.VMEM)
    out, slip = pl.pallas_call(
        functools.partial(kernel, (nx, ny, points)),
        out_shape=(
            jax.ShapeDtypeStruct(wavefield.shape, F32),
            jax.ShapeDtypeStruct((1, owned), F32),
        ),
        in_specs=[pl.BlockSpec(memory_space=pl.ANY)] * 7 + [vmem] * 10,
        out_specs=(vmem, vmem),
        scratch_shapes=[pltpu.VMEM(x.shape, F32) for x in fetched]
        + [field] * 6
        + [
            pltpu.VMEM((3 * modes, VARS * elems), F32),
            pltpu.VMEM((VARS * rows, 4 * elems), F32),
            pltpu.VMEM((VARS * rows, 4 * elems), F32),
            pltpu.VMEM((4 * rows, VARS * elems), F32),
            pltpu.VMEM((4 * rows, modes), F32),
            pltpu.VMEM((3 * modes, 3 * modes), BF16),
            pltpu.VMEM((3 * modes, 3 * modes), BF16),
            pltpu.VMEM((4 * rows, 3 * modes), BF16),
            pltpu.VMEM((modes, 12 * rows), BF16),
            pltpu.VMEM((4 * elems + 4 * slot_count, 4 * elems), BF16),
            pltpu.VMEM((4 * elems, 4 * slot_count), BF16),
            pltpu.VMEM((4 * elems, count), F32),
            pltpu.VMEM((owned, count), F32),
            pltpu.VMEM((ny, 8, owned), F32),
            pltpu.VMEM((8, 4 * elems), F32),
            pltpu.VMEM((8, 4 * elems), F32),
            pltpu.VMEM((ny, 8, owned), F32),
            pltpu.VMEM((ny, 8, owned), F32),
            pltpu.VMEM((2, 4, group, 4 * slot_count), F32),
            pltpu.VMEM((2, 4, group, 4 * slot_count), F32),
            pltpu.VMEM((4 * group, 4 * slot_count), F32),
            pltpu.SemaphoreType.DMA((ny,)),
            pltpu.SemaphoreType.DMA((ny,)),
            pltpu.SemaphoreType.DMA((ny,)),
            pltpu.SemaphoreType.DMA((ny,)),
            pltpu.SemaphoreType.DMA((2, 4)),
            pltpu.SemaphoreType.DMA((2, 4)),
            pltpu.SemaphoreType.DMA((len(fetched),)),
        ],
        compiler_params=pltpu.CompilerParams(
            collective_id=0, has_side_effects=True, vmem_limit_bytes=60 * 1024 * 1024
        ),
    )(
        *fetched,
        cluster.reshape(1, elems),
        yield_stress.reshape(1, elems),
        plastic_mask.reshape(1, elems),
        face_source,
        send_faces,
        fault_faces,
        fault_owner.reshape(1, count),
        fault_slip.reshape(1, owned),
        cohesion.reshape(1, owned),
        slip_flag.reshape(1, owned),
    )
    return (out, slip.reshape(owned))


def solution(mesh):
    both = ("gx", "gy")
    return jax.shard_map(
        functools.partial(local, mesh.shape["gx"], mesh.shape["gy"]),
        mesh=mesh,
        in_specs=(
            P(None, None, both),
            P(None, None, None, both),
            P(None, None, None, both),
            P(None, None, None, both),
            P(),
            P(),
            P(),
            P(both),
            P(both),
            P(both),
            P(None, both),
            P(both, None),
            P(both, None),
            P(both, None),
            P(both),
            P(both),
            P(both),
        ),
        out_specs=(P(None, None, both), P(both)),
        check_vma=False,
    )
```
